256 devices in a mesh: dp: 16 (over z_lo, x), ctx: 16 (over z_hi, y, core).
Axes of the slice: x: 4, y: 4, z: 8 (z_hi: 2, z_lo: 4; z = z_hi * 4 + z_lo), core: 2. Of those that a mesh axis runs over, the one named last changes fastest.
Arguments:
- long_query: bfloat16 [16, 1536, 4096], P('dp', 'ctx'), may hold values from -5 to 5
- long_key: bfloat16 [16, 1536, 512], P('dp', 'ctx'), may hold values from -5 to 5
- long_value: bfloat16 [16, 1536, 512], P('dp', 'ctx'), may hold values from -6 to 6
- long_cotangent: bfloat16 [16, 1536, 4096], P('dp', 'ctx'), may hold values from -6 to 6
- block_order: int32 [16, 32], P('dp'), may hold values from 0 to 31, each once within a row
- short_query: bfloat16 [16, 1024, 4096], P('dp', 'ctx'), may hold values from -5 to 5
- short_key: bfloat16 [16, 1024, 512], P('dp', 'ctx'), may hold values from -5 to 5
- short_value: bfloat16 [16, 1024, 512], P('dp', 'ctx'), may hold values from -6 to 6
- short_cotangent: bfloat16 [16, 1024, 4096], P('dp', 'ctx'), may hold values from -6 to 6
- doc_lengths: int32 [16, 16, 4], P(None, 'ctx'), may hold values from 1 to 32, 64 in all within a row
- balance_list: int32 [16, 16], P('ctx'), may hold values from 0 to 15, as said below
Outputs:
- long_output: bfloat16 [16, 1536, 4096], P('dp', 'ctx')
- long_query_grad: bfloat16 [16, 1536, 4096], P('dp', 'ctx')
- long_key_grad: bfloat16 [16, 1536, 512], P('dp', 'ctx')
- long_value_grad: bfloat16 [16, 1536, 512], P('dp', 'ctx')
- short_output: bfloat16 [16, 1024, 4096], P('dp', 'ctx')
- short_query_grad: bfloat16 [16, 1024, 4096], P('dp', 'ctx')
- short_key_grad: bfloat16 [16, 1024, 512], P('dp', 'ctx')
- short_value_grad: bfloat16 [16, 1024, 512], P('dp', 'ctx')
The draws below stay inside these ranges and needn't reach their ends.
Inputs may be any that keep to these rules, and one draw needn't show every extreme that they name: `block_order`: each row is a permutation of 0 to 31. `balance_list`: row c maps each data group j to j XOR m_c, for one number m_c of 0 to 15 per row; in some row m_c = 15, and in another row m_c = 8. `doc_lengths`: the lengths of a pack sum to 64; the longest is exactly 32.
All inputs are finite; a program needn't handle non-finite values.
Results may differ from the reference program's by a relative error of at most 0.012.
Values may be sent and summed in bfloat16 or wider, within the bound.
A program may use at most 128 MiB of HBM per device.

```python
import math
import jax
import jax.numpy as jnp
import numpy as np
from jax import lax

HD = 128
Q_HEADS = 32
KV_HEADS = 4
LONG_DEV = 96
SHORT_DEV = 64
DOCS = 4
SHORT_MOST = 32
LONG_LEN = 1536
N_DP = 16
N_CTX = 16


def query_values(key, salt, count_rows):
    key = jax.random.fold_in(key, salt + 3)
    values = jnp.clip(jax.random.normal(key, (N_DP, count_rows, Q_HEADS * HD), jnp.float32), -5.0, 5.0)
    return values.astype(jnp.bfloat16)


def key_values(key, salt, count_rows):
    key = jax.random.fold_in(key, salt + 5)
    values = jnp.clip(jax.random.normal(key, (N_DP, count_rows, KV_HEADS * HD), jnp.float32), -5.0, 5.0)
    return values.astype(jnp.bfloat16)


def draw_long_query(key, part):
    return query_values(key, 17, N_CTX * LONG_DEV)


def draw_long_key(key, part):
    return key_values(key, 17, N_CTX * LONG_DEV)


def draw_short_query(key, part):
    return query_values(key, 29, N_CTX * SHORT_DEV)


def draw_short_key(key, part):
    return key_values(key, 29, N_CTX * SHORT_DEV)


def draw_balance_list(key, part):
    key = jax.random.fold_in(key, 41)
    masks = jax.random.randint(jax.random.fold_in(key, 1), (N_CTX,), 0, N_DP, jnp.int32)
    full_row = jax.random.randint(jax.random.fold_in(key, 2), (), 0, N_CTX, jnp.int32)
    step_away = jax.random.randint(jax.random.fold_in(key, 3), (), 1, N_CTX, jnp.int32)
    half_row = (full_row + step_away) % N_CTX
    columns = jnp.arange(N_CTX, dtype=jnp.int32)
    masks = jnp.where(columns == full_row, N_DP - 1, masks)
    masks = jnp.where(columns == half_row, N_DP // 2, masks)
    return jnp.bitwise_xor(jnp.arange(N_DP, dtype=jnp.int32)[None, :], masks[:, None]).astype(jnp.int32)


def steps_of(rng, dims, split, least, top_value):
    gain = 1.0
    for position, parts in split:
        steps = jax.random.uniform(jax.random.fold_in(jax.random.fold_in(rng, 6), position), (parts,), jnp.float32, least / len(split), top_value / len(split))
        gain = gain * jnp.repeat(jnp.exp(steps), dims[position] // parts).reshape((-1,) + (1,) * (len(dims) - 1 - position))
    return gain


def length_profile(number_of, total, limit, slope):
    loads = [(1 << 20) // math.isqrt(rank ** slope) + 1 for rank in range(2, number_of + 1)]
    spare, holding = total - limit - (number_of - 1), [1] * (number_of - 1)
    while spare > 0:
        free = [i for i in range(number_of - 1) if holding[i] < limit]
        mass, budget = sum([loads[i] for i in free]), spare
        for i in free:
            addition = min(limit - holding[i], max(1, budget * loads[i] // mass), spare)
            holding[i] = holding[i] + addition
            spare = spare - addition
    return np.array([limit] + holding)


def uneven(own_key, amount, total, bound, skew):
    if amount == 2:
        one = jax.random.randint(own_key, (), max(1, total - bound), min(bound, total - 1) + 1)
        return jnp.stack([one, total - one])
    lengths = jnp.asarray(length_profile(amount, total, bound, skew), jnp.int32)
    pairs = (amount - 1) // 2
    source_of, sink = lengths[1:1 + 2 * pairs:2], lengths[2:2 + 2 * pairs:2]
    margin = jnp.minimum(source_of - 1, bound - sink)
    moved = jax.random.randint(jax.random.fold_in(own_key, 1), (pairs,), 0, 1 << 20) % (margin + 1)
    lengths = lengths.at[1:1 + 2 * pairs:2].set(source_of - moved).at[2:2 + 2 * pairs:2].set(sink + moved)
    return lengths[jax.random.permutation(jax.random.fold_in(own_key, 2), amount)]


def noise(key, dims, scale, reach, pieces=(), held_as=jnp.bfloat16):
    array = scale * jax.random.normal(key, dims, jnp.float32)
    if pieces:
        array = array * steps_of(key, dims, pieces, -0.22, 0.18)
    return jnp.clip(array, -reach, reach).astype(held_as)


def setup_inputs(seed: int = 0) -> dict:
    keys = jax.random.split(jax.random.key(seed), 12)
    return {
        "long_query": draw_long_query(jax.random.fold_in(keys[11], 71), 0),
        "long_key": draw_long_key(jax.random.fold_in(keys[11], 71), 0),
        "long_value": noise(keys[2], (N_DP, LONG_LEN, KV_HEADS * HD), 1.0, 6.0, ((0, 16), (1, 16))),
        "long_cotangent": noise(keys[3], (N_DP, LONG_LEN, Q_HEADS * HD), 1.0, 6.0, ((0, 16), (1, 16))),
        "block_order": jax.vmap(lambda own: jax.random.permutation(own, 2 * N_CTX))(jax.random.split(keys[4], N_DP)).reshape((N_DP, 2 * N_CTX)).astype(jnp.int32),
        "short_query": draw_short_query(jax.random.fold_in(keys[11], 71), 0),
        "short_key": draw_short_key(jax.random.fold_in(keys[11], 71), 0),
        "short_value": noise(keys[7], (N_DP, N_CTX * SHORT_DEV, KV_HEADS * HD), 1.0, 6.0, ((0, 16), (1, 16))),
        "short_cotangent": noise(keys[8], (N_DP, N_CTX * SHORT_DEV, Q_HEADS * HD), 1.0, 6.0, ((0, 16), (1, 16))),
        "doc_lengths": jax.vmap(lambda own: uneven(own, DOCS, SHORT_DEV, SHORT_MOST, 2))(jax.random.split(keys[9], N_DP * N_CTX)).reshape((N_DP, N_CTX, DOCS)).astype(jnp.int32),
        "balance_list": draw_balance_list(jax.random.fold_in(keys[11], 71), 0),
    }


def attend(queries, keyset, valueset, cotangent, allowed):
    scale_factor = HD ** -0.5
    query_float = queries.astype(jnp.float32)
    key_float = keyset.astype(jnp.float32)
    value_float = valueset.astype(jnp.float32)
    cot_float = cotangent.astype(jnp.float32)
    scores = jnp.einsum("rgd,kd->grk", query_float, key_float) * scale_factor
    masked = jnp.where(allowed[None], scores, -1e30)
    highest = jnp.max(masked, axis=2, keepdims=True)
    total = jnp.sum(jnp.exp(masked - highest), axis=2, keepdims=True)
    probs = jnp.exp(masked - highest - jnp.log(total))
    probs_low = lax.optimization_barrier(probs.astype(jnp.bfloat16))
    probs_back = probs_low.astype(jnp.float32)
    output = lax.optimization_barrier(jnp.einsum("grk,kd->rgd", probs_back, value_float).astype(jnp.bfloat16))
    deltas = jnp.sum(cot_float * output.astype(jnp.float32), axis=2)
    dprobs = jnp.einsum("rgd,kd->grk", cot_float, value_float)
    dscores = probs * (dprobs - jnp.transpose(deltas)[:, :, None])
    dscore_low = lax.optimization_barrier(dscores.astype(jnp.bfloat16))
    dscore_back = dscore_low.astype(jnp.float32)
    query_grad = (jnp.einsum("grk,kd->rgd", dscore_back, key_float) * scale_factor).astype(jnp.bfloat16)
    key_grad = jnp.einsum("grk,rgd->kd", dscore_back, query_float) * scale_factor
    value_grad = jnp.einsum("grk,rgd->kd", probs_back, cot_float)
    return output, query_grad, key_grad, value_grad


def all_heads(query_rows, key_rows, value_rows, cot_rows, allowed):
    group_size = Q_HEADS // KV_HEADS
    row_count = query_rows.shape[0]
    key_count = key_rows.shape[0]
    queries = query_rows.reshape(row_count, KV_HEADS, group_size, HD)
    cotangents = cot_rows.reshape(row_count, KV_HEADS, group_size, HD)
    key_heads = key_rows.reshape(key_count, KV_HEADS, HD)
    value_heads = value_rows.reshape(key_count, KV_HEADS, HD)
    outputs, query_grads, key_grads, value_grads = [], [], [], []
    for head_group in range(KV_HEADS):
        output, query_grad, key_grad, value_grad = attend(queries[:, head_group], key_heads[:, head_group], value_heads[:, head_group], cotangents[:, head_group], allowed)
        outputs.append(output)
        query_grads.append(query_grad)
        key_grads.append(key_grad)
        value_grads.append(value_grad)
    output = jnp.stack(outputs, axis=1).reshape(row_count, Q_HEADS * HD)
    query_grad = jnp.stack(query_grads, axis=1).reshape(row_count, Q_HEADS * HD)
    key_grad = jnp.stack(key_grads, axis=1).reshape(key_count, KV_HEADS * HD).astype(jnp.bfloat16)
    value_grad = jnp.stack(value_grads, axis=1).reshape(key_count, KV_HEADS * HD).astype(jnp.bfloat16)
    return output, query_grad, key_grad, value_grad


def reference(long_query, long_key, long_value, long_cotangent, block_order, short_query, short_key, short_value, short_cotangent, doc_lengths, balance_list):
    block = LONG_DEV // 2

    def long_group(operands):
        query_rows, key_rows, value_rows, cot_rows, ordering = operands
        positions = (ordering[:, None] * block + jnp.arange(block, dtype=jnp.int32)[None, :]).reshape(-1)
        allowed = positions[:, None] >= positions[None, :]
        return all_heads(query_rows, key_rows, value_rows, cot_rows, allowed)

    long_results = lax.map(long_group, (long_query, long_key, long_value, long_cotangent, block_order))

    def short_pack(flat):
        dest_group = (flat // N_CTX).astype(jnp.int32)
        column = (flat % N_CTX).astype(jnp.int32)
        targets = lax.dynamic_index_in_dim(balance_list, column, 0, keepdims=False)
        source = jnp.sum(jnp.where(targets == dest_group, jnp.arange(N_DP, dtype=jnp.int32), 0)).astype(jnp.int32)
        first = (column * SHORT_DEV).astype(jnp.int32)
        zero_index = jnp.zeros((), jnp.int32)
        query_rows = lax.dynamic_slice(short_query, (source, first, zero_index), (1, SHORT_DEV, Q_HEADS * HD))[0]
        key_rows = lax.dynamic_slice(short_key, (source, first, zero_index), (1, SHORT_DEV, KV_HEADS * HD))[0]
        value_rows = lax.dynamic_slice(short_value, (source, first, zero_index), (1, SHORT_DEV, KV_HEADS * HD))[0]
        cot_rows = lax.dynamic_slice(short_cotangent, (dest_group, first, zero_index), (1, SHORT_DEV, Q_HEADS * HD))[0]
        doc_sizes = lax.dynamic_slice(doc_lengths, (source, column, zero_index), (1, 1, DOCS))[0, 0]
        doc_ends = jnp.cumsum(doc_sizes)
        steps_rows = jnp.arange(SHORT_DEV, dtype=jnp.int32)
        doc_ids = jnp.sum((steps_rows[:, None] >= doc_ends[None, :]).astype(jnp.int32), axis=1)
        allowed = (doc_ids[:, None] == doc_ids[None, :]) & (steps_rows[:, None] >= steps_rows[None, :])
        return all_heads(query_rows, key_rows, value_rows, cot_rows, allowed)

    short_results = lax.map(short_pack, jnp.arange(N_DP * N_CTX, dtype=jnp.int32))
    short_shaped = [member.reshape(N_DP, N_CTX * SHORT_DEV, member.shape[-1]) for member in short_results]
    return (long_results[0], long_results[1], long_results[2], long_results[3], short_shaped[0], short_shaped[1], short_shaped[2], short_shaped[3])
```

```python
import jax
import jax.numpy as jnp
from jax import lax
from jax.experimental import pallas as pl
from jax.experimental.pallas import tpu as pltpu
from jax.sharding import PartitionSpec as P

HD = 128
GROUP = 8
KV_HEADS = 4
ROWS = 96
BLOCK = 48
KEYS = 1536
SHORT = 64
TILE = 256
TILES = KEYS // TILE
N_DP = 16
SCALE = HD**-0.5
LOG2E = 1.4426950408889634
NT = (((1,), (1,)), ((), ()))
F32 = jnp.float32
BF16 = jnp.bfloat16
MESH = pl.DeviceIdType.MESH


def dot(a, b):
    return jnp.dot(a, b, preferred_element_type=F32)


def dot_nt(a, b):
    return lax.dot_general(a, b, NT, preferred_element_type=F32)


def kernel(
    lq, lk, lv, lc, bo, sq, sk, sv, sc, dl, bl,
    lo, ldq, ldk, ldv, so, sdq, sdk, sdv,
    kv, kvx, qb, cb, qh, ch, oh, dqh, ob, dqb, kmat, vmat, ktr, vtr, qps, sbuf, pbuf, acc,
    rs_s, rs_r, rz_o, rz_s, rz_r, rfin,
    st, r1, s2, r2, qs, cs, ks, vs,
    ag_send, ag_recv, qx_send, qx_recv, loc, p1_send, p1_recv, p2_send, p2_recv,
    ry_send, ry_recv, rz_send, rz_recv, fin_send, fin_recv, out_send, out_recv,
):
    d = lax.axis_index("dp")
    c = lax.axis_index("ctx")
    h = c % 2
    y = (c // 2) % 4
    zh = c // 8
    sib = {"ctx": c + 1 - 2 * h}
    anti = {"ctx": (c + 8) % 16}

    def at_y(k):
        return {"ctx": zh * 8 + ((y + k) % 4) * 2 + h}

    def at_dp(k):
        return {"dp": (d + k) % N_DP}

    def remote(src, dst, send, recv, to):
        return pltpu.make_async_remote_copy(
            src_ref=src, dst_ref=dst, send_sem=send, recv_sem=recv, device_id=to, device_id_type=MESH
        )

    barrier = pltpu.get_barrier_semaphore()
    peers = [sib, anti] + [at_y(k) for k in range(1, 4)] + [at_dp(k) for k in range(1, N_DP)]
    for peer in peers:
        pl.semaphore_signal(barrier, inc=1, device_id=peer, device_id_type=MESH)

    mine = pl.ds(pl.multiple_of(h * 256, 256), 256)
    other = pl.ds(pl.multiple_of((1 - h) * 256, 256), 256)
    kv[zh, y, h, 0] = lk[0, :, mine]
    kv[zh, y, h, 1] = lv[0, :, mine]
    kvx[0] = lk[0, :, other]
    kvx[1] = lv[0, :, other]
    for a in range(4):
        for b in range(4):
            rows = slice(16 * a, 16 * a + 16)
            st[4 * a + b, :, 0:1024] = sq[0, rows, 1024 * b : 1024 * b + 1024]
            st[4 * a + b, :, 1024:1152] = sk[0, rows, 128 * b : 128 * b + 128]
            st[4 * a + b, :, 1152:1280] = sv[0, rows, 128 * b : 128 * b + 128]
    r1[0] = st[0]
    for part in range(3):
        column = lax.broadcasted_iota(jnp.int32, (1, TILE), 1) + part * TILE
        position = jnp.zeros((1, TILE), jnp.int32)
        for k in range(16):
            start = bo[0, zh * 16 + y * 4 + k % 4] * BLOCK - BLOCK * k
            position = jnp.where(column >= BLOCK * k, column + start, position)
        qps[part] = position

    pl.semaphore_wait(barrier, len(peers))

    waits = []

    def begin(copy):
        copy.start()
        waits.append(copy)
        return copy

    sib_kv = begin(remote(kvx, kv.at[zh, y, h], ag_send.at[0], ag_recv.at[0], sib))
    wide_mine = pl.ds(pl.multiple_of(h * 2048, 2048), 2048)
    wide_other = pl.ds(pl.multiple_of((1 - h) * 2048, 2048), 2048)
    sib_q = begin(remote(lq.at[0, :, wide_other], qb.at[h], qx_send.at[0], qx_recv.at[0], sib))
    sib_c = begin(remote(lc.at[0, :, wide_other], cb.at[h], qx_send.at[1], qx_recv.at[1], sib))
    own_q = pltpu.make_async_copy(lq.at[0, :, wide_mine], qb.at[h], loc.at[0])
    own_c = pltpu.make_async_copy(lc.at[0, :, wide_mine], cb.at[h], loc.at[1])
    own_q.start()
    own_c.start()
    sib_kv.wait_recv()
    zcopy = begin(remote(kv.at[zh, y], kv.at[zh, y], ag_send.at[1], ag_recv.at[1], anti))
    up = begin(remote(kv.at[zh, y], kv.at[zh, y], ag_send.at[2], ag_recv.at[2], at_y(1)))
    down = begin(remote(kv.at[zh, y], kv.at[zh, y], ag_send.at[3], ag_recv.at[3], at_y(3)))
    first = [
        begin(remote(st.at[p], r1.at[p], p1_send.at[p], p1_recv.at[p], at_dp(p)))
        for p in range(1, N_DP)
    ]
    own_q.wait()
    own_c.wait()
    sib_q.wait_recv()
    sib_c.wait_recv()
    for g in range(2):
        for j in range(GROUP):
            for r in range(2):
                to = slice(j * 192 + r * ROWS, j * 192 + r * ROWS + ROWS)
                at = slice((g * GROUP + j) * HD, (g * GROUP + j + 1) * HD)
                qh[g, to, :] = qb[r, :, at]
                ch[g, to, :] = cb[r, :, at]
    ylow, yhigh = (y + 3) % 4, (y + 1) % 4
    up.wait_recv()
    relay0 = begin(
        remote(kv.at[zh, ylow, 0], kv.at[zh, ylow, 0], ag_send.at[4], ag_recv.at[4], at_y(1))
    )
    down.wait_recv()
    relay1 = begin(
        remote(kv.at[zh, yhigh, 1], kv.at[zh, yhigh, 1], ag_send.at[5], ag_recv.at[5], at_y(3))
    )
    zcopy.wait_recv()
    zo = 1 - zh
    up2 = begin(remote(kv.at[zo, y], kv.at[zo, y], ag_send.at[6], ag_recv.at[6], at_y(1)))
    down2 = begin(remote(kv.at[zo, y], kv.at[zo, y], ag_send.at[7], ag_recv.at[7], at_y(3)))
    up2.wait_recv()
    relay2 = begin(
        remote(kv.at[zo, ylow, 0], kv.at[zo, ylow, 0], ag_send.at[8], ag_recv.at[8], at_y(1))
    )
    down2.wait_recv()
    relay3 = begin(
        remote(kv.at[zo, yhigh, 1], kv.at[zo, yhigh, 1], ag_send.at[9], ag_recv.at[9], at_y(3))
    )
    for copy in (relay0, relay1, relay2, relay3):
        copy.wait_recv()

    sub = lax.broadcasted_iota(jnp.int32, (BLOCK, TILE), 0)

    def attend(g):
        kmat[...] = kv[:, :, :, 0, :, g * HD : (g + 1) * HD].reshape(KEYS, HD)
        vmat[...] = kv[:, :, :, 1, :, g * HD : (g + 1) * HD].reshape(KEYS, HD)
        ktr[...] = kmat[...].T
        vtr[...] = vmat[...].T
        acc[...] = jnp.zeros_like(acc)

        def tile(t, carry):
            rows = pl.ds(pl.multiple_of(t * TILE, TILE), TILE)
            qt = qh[g, rows, :]
            ct = ch[g, rows, :]
            qp = qps[t % 3]
            s = dot_nt(kmat[...], qt)
            top = jnp.full((8, TILE), -1e30, F32)
            for b in range(KEYS // BLOCK):
                at = slice(b * BLOCK, (b + 1) * BLOCK)
                block = jnp.where(sub <= qp - bo[0, b] * BLOCK, s[at] * (SCALE * LOG2E), -1e30)
                sbuf[at, :] = block
                top = jnp.maximum(top, jnp.max(block.reshape(6, 8, TILE), axis=0))
            top = jnp.max(top, axis=0, keepdims=True)
            total = jnp.zeros((8, TILE), F32)
            for b in range(KEYS // BLOCK):
                at = slice(b * BLOCK, (b + 1) * BLOCK)
                block = jnp.exp2(sbuf[at, :] - top)
                sbuf[at, :] = block
                total = total + jnp.sum(block.reshape(6, 8, TILE), axis=0)
            inverse = 1.0 / jnp.sum(total, axis=0, keepdims=True)
            for b in range(KEYS // BLOCK):
                at = slice(b * BLOCK, (b + 1) * BLOCK)
                pbuf[at, :] = (sbuf[at, :] * inverse).astype(BF16)
            out = dot(vtr[...], pbuf[...])
            acc[:, HD:] += dot(pbuf[...], ct)
            oh[g, rows, :] = out.T.astype(BF16)
            delta = jnp.sum(out.astype(BF16).astype(F32) * ct.astype(F32).T, axis=0, keepdims=True)
            dprobs = dot_nt(vmat[...], ct)
            for b in range(KEYS // BLOCK):
                at = slice(b * BLOCK, (b + 1) * BLOCK)
                pbuf[at, :] = (sbuf[at, :] * ((dprobs[at] - delta) * inverse)).astype(BF16)
            dq = dot(ktr[...], pbuf[...])
            acc[:, :HD] += dot(pbuf[...], qt)
            dqh[g, rows, :] = (dq * SCALE).T.astype(BF16)
            return carry

        lax.fori_loop(0, TILES, tile, 0)

    def give(g):
        for z in range(2):
            for row in range(4):
                part = acc[(z * 4 + row) * 192 : (z * 4 + row + 1) * 192, :]
                rs_s[g, row, z, :, :, :HD] = (part[:, :HD] * SCALE).astype(BF16).reshape(2, ROWS, HD)
                rs_s[g, row, z, :, :, HD:] = part[:, HD:].astype(BF16).reshape(2, ROWS, HD)
        copies = [
            begin(
                remote(
                    rs_s.at[g, (y + k) % 4],
                    rs_r.at[g, k - 1],
                    ry_send.at[3 * g + k - 1],
                    ry_recv.at[3 * g + k - 1],
                    at_y(k),
                )
            )
            for k in range(1, 4)
        ]
        for j in range(GROUP):
            for r in range(2):
                at = slice(j * 192 + r * ROWS, j * 192 + r * ROWS + ROWS)
                ob[g, r, :, j * HD : (j + 1) * HD] = oh[g, at, :]
                dqb[g, r, :, j * HD : (j + 1) * HD] = dqh[g, at, :]
        place = pl.ds(pl.multiple_of(h * 2048 + g * 1024, 1024), 1024)
        outs = []
        for i, (source, target) in enumerate(((ob, lo), (dqb, ldq))):
            begin_at = 2 * g + i
            outs.append(
                begin(
                    remote(
                        source.at[g, 1 - h],
                        target.at[0, :, place],
                        out_send.at[begin_at],
                        out_recv.at[begin_at],
                        sib,
                    )
                )
            )
            own = pltpu.make_async_copy(
                source.at[g, h], target.at[0, :, place], loc.at[2 + begin_at]
            )
            own.start()
            outs.append(own)
        return copies, outs

    attend(0)
    mask = bl[0, 0]
    for copy in first:
        copy.wait_recv()
    for k in range(N_DP):
        s2[k] = r1[(d - ((d + k) % N_DP ^ mask) + N_DP) % N_DP]
    r2[0] = s2[0]
    second = [
        begin(remote(s2.at[k], r2.at[k], p2_send.at[k], p2_recv.at[k], at_dp(k)))
        for k in range(1, N_DP)
    ]
    copies0, outs0 = give(0)
    attend(1)
    copies1, outs1 = give(1)

    def reduce_y(g, copies):
        for copy in copies:
            copy.wait_recv()
        def total(z):
            value = rs_s[g, y, z].astype(F32)
            for k in range(3):
                value = value + rs_r[g, k, z].astype(F32)
            return value
        rz_s[g] = total(1 - zh).astype(BF16)
        sent = begin(remote(rz_s.at[g], rz_r.at[g], rz_send.at[g], rz_recv.at[g], anti))
        rz_o[g] = total(zh)
        return sent

    def reduce_z(g, sent):
        sent.wait_recv()
        rfin[g] = (rz_o[g] + rz_r[g].astype(F32)).astype(BF16)
        place = pl.ds(pl.multiple_of(h * 256 + g * HD, HD), HD)
        finals = []
        for i, target in enumerate((ldk, ldv)):
            at = 2 * g + i
            lanes = pl.ds(i * HD, HD)
            finals.append(
                begin(
                    remote(
                        rfin.at[g, 1 - h, :, lanes],
                        target.at[0, :, place],
                        fin_send.at[at],
                        fin_recv.at[at],
                        sib,
                    )
                )
            )
            own = pltpu.make_async_copy(
                rfin.at[g, h, :, lanes], target.at[0, :, place], loc.at[6 + at]
            )
            own.start()
            finals.append(own)
        return finals

    z0 = reduce_y(0, copies0)
    for copy in second:
        copy.wait_recv()
    z1 = reduce_y(1, copies1)

    source = d ^ mask
    base = d - source + 2 * N_DP
    for a in range(4):
        for b in range(4):
            piece = r2[(base - (4 * a + b)) % N_DP]
            ks[b, 16 * a : 16 * a + 16, :] = piece[:, 1024:1152]
            vs[b, 16 * a : 16 * a + 16, :] = piece[:, 1152:1280]
            for j in range(GROUP):
                qs[b, j * SHORT + 16 * a : j * SHORT + 16 * a + 16, :] = piece[
                    :, j * HD : (j + 1) * HD
                ]
    width = GROUP * SHORT
    for b in range(4):
        for j in range(GROUP):
            at = (b * GROUP + j) * HD
            cs[b, j * SHORT : (j + 1) * SHORT, :] = sc[0, :, at : at + HD]
    key_row = lax.broadcasted_iota(jnp.int32, (SHORT, width), 0)
    query_row = lax.broadcasted_iota(jnp.int32, (SHORT, width), 1) & (SHORT - 1)
    key_doc = jnp.zeros((SHORT, width), jnp.int32)
    query_doc = jnp.zeros((SHORT, width), jnp.int32)
    end = jnp.int32(0)
    for k in range(4):
        end = end + dl[source, 0, k]
        key_doc = key_doc + jnp.where(key_row >= end, 1, 0)
        query_doc = query_doc + jnp.where(query_row >= end, 1, 0)
    allowed = (key_doc == query_doc) & (key_row <= query_row)
    for b in range(KV_HEADS):
        qt, ct, kt, vt = qs[b], cs[b], ks[b], vs[b]
        s = jnp.where(allowed, dot_nt(kt, qt) * (SCALE * LOG2E), -1e30)
        s = jnp.exp2(s - jnp.max(s, axis=0, keepdims=True))
        probs = s * (1.0 / jnp.sum(s, axis=0, keepdims=True))
        low = probs.astype(BF16)
        out = dot(vt.astype(F32).T.astype(BF16), low)
        sdv[0, :, b * HD : (b + 1) * HD] = dot(low, ct).astype(BF16)
        delta = jnp.sum(out.astype(BF16).astype(F32) * ct.astype(F32).T, axis=0, keepdims=True)
        ds = (probs * (dot_nt(vt, ct) - delta)).astype(BF16)
        dq = dot(kt.astype(F32).T.astype(BF16), ds) * SCALE
        sdk[0, :, b * HD : (b + 1) * HD] = (dot(ds, qt) * SCALE).astype(BF16)
        out = out.T.astype(BF16)
        dq = dq.T.astype(BF16)
        for j in range(GROUP):
            at = (b * GROUP + j) * HD
            so[0, :, at : at + HD] = out[j * SHORT : (j + 1) * SHORT]
            sdq[0, :, at : at + HD] = dq[j * SHORT : (j + 1) * SHORT]

    finals = reduce_z(0, z0) + reduce_z(1, z1)
    for copy in outs0[1::2] + outs1[1::2] + finals[1::2]:
        copy.wait()
    for copy in outs0[0::2] + outs1[0::2] + finals[0::2]:
        copy.wait_recv()
    for copy in waits:
        copy.wait_send()


def per_device(*args):
    any_spec = pl.BlockSpec(memory_space=pl.ANY)
    vmem = pl.BlockSpec(memory_space=pltpu.VMEM)
    smem = pl.BlockSpec(memory_space=pltpu.SMEM)
    dma = pltpu.SemaphoreType.DMA
    long_query, long_key, short_query, short_key = args[0], args[1], args[5], args[6]

    def shape(like):
        return jax.ShapeDtypeStruct(like.shape, like.dtype)

    def buffer(*dims, dtype=BF16):
        return pltpu.VMEM(dims, dtype)

    return pl.pallas_call(
        kernel,
        out_shape=(
            shape(long_query), shape(long_query), shape(long_key), shape(long_key),
            shape(short_query), shape(short_query), shape(short_key), shape(short_key),
        ),
        in_specs=[any_spec, vmem, vmem, any_spec, smem, vmem, vmem, vmem, vmem, smem, smem],
        out_specs=(any_spec,) * 4 + (vmem,) * 4,
        scratch_shapes=[
            buffer(2, 4, 2, 2, ROWS, 256),
            buffer(2, ROWS, 256),
            buffer(2, ROWS, 2048),
            buffer(2, ROWS, 2048),
            buffer(2, KEYS, HD),
            buffer(2, KEYS, HD),
            buffer(2, KEYS, HD),
            buffer(2, KEYS, HD),
            buffer(2, 2, ROWS, 1024),
            buffer(2, 2, ROWS, 1024),
            buffer(KEYS, HD),
            buffer(KEYS, HD),
            buffer(HD, KEYS),
            buffer(HD, KEYS),
            buffer(3, 1, TILE, dtype=jnp.int32),
            buffer(KEYS, TILE, dtype=F32),
            buffer(KEYS, TILE),
            buffer(KEYS, 256, dtype=F32),
            buffer(2, 4, 2, 2, ROWS, 256),
            buffer(2, 3, 2, 2, ROWS, 256),
            buffer(2, 2, ROWS, 256, dtype=F32),
            buffer(2, 2, ROWS, 256),
            buffer(2, 2, ROWS, 256),
            buffer(2, 2, ROWS, 256),
            buffer(N_DP, 16, 1280),
            buffer(N_DP, 16, 1280),
            buffer(N_DP, 16, 1280),
            buffer(N_DP, 16, 1280),
            buffer(4, GROUP * SHORT, HD),
            buffer(4, GROUP * SHORT, HD),
            buffer(4, SHORT, HD),
            buffer(4, SHORT, HD),
            dma((10,)), dma((10,)), dma((2,)), dma((2,)), dma((10,)),
            dma((N_DP,)), dma((N_DP,)), dma((N_DP,)), dma((N_DP,)),
            dma((6,)), dma((6,)), dma((2,)), dma((2,)), dma((4,)), dma((4,)), dma((4,)), dma((4,)),
        ],
        compiler_params=pltpu.CompilerParams(
            collective_id=0, has_side_effects=True, vmem_limit_bytes=48 * 1024 * 1024
        ),
    )(*args)


def solution(mesh):
    wide = P("dp", "ctx", None)
    return jax.shard_map(
        per_device,
        mesh=mesh,
        in_specs=(wide,) * 4
        + (P("dp", None),)
        + (wide,) * 4
        + (P(None, "ctx", None), P("ctx", None)),
        out_specs=(wide,) * 8,
        check_vma=False,
    )
```

```python
import jax
import jax.numpy as jnp
from jax import lax
from jax.experimental import pallas as pl
from jax.experimental.pallas import tpu as pltpu
from jax.sharding import PartitionSpec as P

HD = 128
GROUP = 8
KV_HEADS = 4
ROWS = 96
BLOCK = 48
KEYS = 1536
SHORT = 64
TILE = 256
TILES = KEYS // TILE
N_DP = 16
SEMS = 96
VMEM_LIMIT = 62 * 1024 * 1024
FIRST_EARLY = True
FAR_AT = 1
SECOND_AT = 5
SUM_AT = 10
SCALE = HD**-0.5
LOG2E = 1.4426950408889634
NT = (((1,), (1,)), ((), ()))
F32 = jnp.float32
BF16 = jnp.bfloat16
MESH = pl.DeviceIdType.MESH


def dot(a, b):
    return jnp.dot(a, b, preferred_element_type=F32)


def dot_nt(a, b):
    return lax.dot_general(a, b, NT, preferred_element_type=F32)


def kernel(
    lq, lk, lv, lc, bo, sq, sk, sv, sc, dl, bl,
    lo, ldq, ldk, ldv, so, sdq, sdk, sdv,
    lkb, lvb, sqb, skb, svb, scb,
    kv, kvx, qb, cb, qh, ch, oh, dqh, ob, dqb, kmat, vmat, ktr, vtr, qps, sbuf, pbuf, acc,
    rs_s, rs_r, rz_o, rz_s, rz_r, rfin,
    st, r1, s2, r2, qs, cs, ks, vs,
    loc, sends, recvs,
):
    d = lax.axis_index("dp")
    c = lax.axis_index("ctx")
    h = c % 2
    y = (c // 2) % 4
    zh = c // 8
    zo = 1 - zh
    ylow, yhigh = (y + 3) % 4, (y + 1) % 4
    sib = {"ctx": c + 1 - 2 * h}
    anti = {"ctx": (c + 8) % 16}
    mask = bl[0, 0]

    def at_y(k):
        return {"ctx": zh * 8 + ((y + k) % 4) * 2 + h}

    def at_dp(k):
        return {"dp": (d + k) % N_DP}

    numbers = {}

    def remote(name, src, dst, to):
        number = numbers.setdefault(name, len(numbers))
        return pltpu.make_async_remote_copy(
            src_ref=src,
            dst_ref=dst,
            send_sem=sends.at[number],
            recv_sem=recvs.at[number],
            device_id=to,
            device_id_type=MESH,
        )

    barrier = pltpu.get_barrier_semaphore()
    peers = [sib, anti] + [at_y(k) for k in range(1, 4)] + [at_dp(k) for k in range(1, N_DP)]
    for peer in peers:
        pl.semaphore_signal(barrier, inc=1, device_id=peer, device_id_type=MESH)

    local = []

    def load(src, dst):
        copy = pltpu.make_async_copy(src, dst, loc.at[len(local)])
        copy.start()
        local.append(copy)
        return copy

    load_k, load_v = load(lk.at[0], lkb), load(lv.at[0], lvb)
    load_s = [load(sq.at[0], sqb), load(sk.at[0], skb), load(sv.at[0], svb)]

    def wide(core, g):
        return pl.ds(pl.multiple_of(core * 2048 + g * 1024, 1024), 1024)

    own_rows = [
        [load(lq.at[0, :, wide(h, g)], qb.at[g, h]), load(lc.at[0, :, wide(h, g)], cb.at[g, h])]
        for g in range(2)
    ]
    load_c = load(sc.at[0], scb)

    for part in range(3):
        column = lax.broadcasted_iota(jnp.int32, (1, TILE), 1) + part * TILE
        position = jnp.zeros((1, TILE), jnp.int32)
        for k in range(16):
            start = bo[0, zh * 16 + y * 4 + k % 4] * BLOCK - BLOCK * k
            position = jnp.where(column >= BLOCK * k, column + start, position)
        qps[part] = position

    load_k.wait()
    load_v.wait()
    for g in range(2):
        mine = pl.ds(pl.multiple_of(h * 256 + g * HD, HD), HD)
        other = pl.ds(pl.multiple_of((1 - h) * 256 + g * HD, HD), HD)
        kv[g, zh, y, h, 0] = lkb[:, mine]
        kv[g, zh, y, h, 1] = lvb[:, mine]
        kvx[g, 0] = lkb[:, other]
        kvx[g, 1] = lvb[:, other]

    pl.semaphore_wait(barrier, len(peers))

    waits = []

    def begin(copy):
        copy.start()
        waits.append(copy)
        return copy

    def same(name, block, to):
        return remote(name, block, block, to)

    sib_kv = [
        begin(remote(f"sib{g}", kvx.at[g], kv.at[g, zh, y, h], sib)) for g in range(2)
    ]
    zc, own_y = [], []
    for g in range(2):
        mine = begin(same(f"z{g}own", kv.at[g, zh, y, h], anti))
        sib_kv[g].wait_recv()
        zc.append([mine, begin(same(f"z{g}sib", kv.at[g, zh, y, 1 - h], anti))])
        own_y.append(
            [
                begin(same(f"up{g}", kv.at[g, zh, y], at_y(1))),
                begin(same(f"down{g}", kv.at[g, zh, y], at_y(3))),
            ]
        )
        if g == 0:
            sib_rows = [
                [
                    begin(remote(f"q{k}", lq.at[0, :, wide(1 - h, k)], qb.at[k, h], sib)),
                    begin(remote(f"c{k}", lc.at[0, :, wide(1 - h, k)], cb.at[k, h], sib)),
                ]
                for k in range(2)
            ]

    def first():
        return [remote(f"first{p}", st.at[p], r1.at[p], at_dp(p)) for p in range(1, N_DP)]

    def second():
        return [remote(f"second{p}", s2.at[p], r2.at[p], at_dp(p)) for p in range(1, N_DP)]

    def begin_first():
        for copy in load_s:
            copy.wait()
        for a in range(4):
            for b in range(4):
                rows = slice(16 * a, 16 * a + 16)
                st[4 * a + b, :, 0:1024] = sqb[rows, 1024 * b : 1024 * b + 1024]
                st[4 * a + b, :, 1024:1152] = skb[rows, 128 * b : 128 * b + 128]
                st[4 * a + b, :, 1152:1280] = svb[rows, 128 * b : 128 * b + 128]
        r1[0] = st[0]
        for copy in first():
            copy.start()

    def begin_second():
        for copy in first():
            copy.wait_recv()
        for k in range(N_DP):
            s2[k] = r1[(d - ((d + k) % N_DP ^ mask) + N_DP) % N_DP]
        r2[0] = s2[0]
        for copy in second():
            copy.start()

    if FIRST_EARLY:
        begin_first()

    def arrange(g):
        for copy in own_rows[g]:
            copy.wait()
        for copy in sib_rows[g]:
            copy.wait_recv()
        for j in range(GROUP):
            for r in range(2):
                to = slice(j * 192 + r * ROWS, j * 192 + r * ROWS + ROWS)
                at = slice(j * HD, (j + 1) * HD)
                qh[g, to, :] = qb[g, r, :, at]
                ch[g, to, :] = cb[g, r, :, at]

    def relays(g, z, name):
        return [
            same(f"relay{g}{name}0", kv.at[g, z, ylow, 0], at_y(1)),
            same(f"relay{g}{name}1", kv.at[g, z, yhigh, 1], at_y(3)),
        ]

    def far_y(g):
        return [
            same(f"upfar{g}", kv.at[g, zo, y], at_y(1)),
            same(f"downfar{g}", kv.at[g, zo, y], at_y(3)),
        ]

    def pass_on(arrived, onward):
        for copy, after in zip(arrived, onward):
            copy.wait_recv()
            after.start()

    arrange(0)
    pass_on(own_y[0], relays(0, zh, "n"))
    for copy in zc[0]:
        copy.wait_recv()
    for copy in far_y(0):
        copy.start()
    pass_on(own_y[1], relays(1, zh, "n"))
    arrange(1)
    pass_on(far_y(0), relays(0, zo, "f"))
    for copy in zc[1]:
        copy.wait_recv()
    for copy in far_y(1):
        copy.start()
    if not FIRST_EARLY:
        begin_first()

    sub = lax.broadcasted_iota(jnp.int32, (BLOCK, TILE), 0)

    def heads(g):
        for copy in relays(g, zh, "n") + relays(g, zo, "f"):
            copy.wait_recv()
        kmat[...] = kv[g, :, :, :, 0].reshape(KEYS, HD)
        vmat[...] = kv[g, :, :, :, 1].reshape(KEYS, HD)
        ktr[...] = kmat[...].T
        vtr[...] = vmat[...].T
        acc[...] = jnp.zeros_like(acc)

    def sums_y(g):
        return [
            remote(f"sum{g}{k}", rs_s.at[g, (y + k) % 4], rs_r.at[g, k - 1], at_y(k))
            for k in (2, 1, 3)
        ]

    def results(g):
        copies, own = [], []
        for i, (source, target) in enumerate(((ob, lo), (dqb, ldq))):
            place = target.at[0, :, wide(h, g)]
            copies.append(remote(f"out{g}{i}", source.at[g, 1 - h], place, sib))
            own.append(pltpu.make_async_copy(source.at[g, h], place, loc.at[16 + 2 * g + i]))
        return copies, own

    def give(g):
        for z in range(2):
            for row in range(4):
                part = acc[(z * 4 + row) * 192 : (z * 4 + row + 1) * 192, :]
                rs_s[g, row, z, :, :, :HD] = (
                    (part[:, :HD] * SCALE).astype(BF16).reshape(2, ROWS, HD)
                )
                rs_s[g, row, z, :, :, HD:] = part[:, HD:].astype(BF16).reshape(2, ROWS, HD)
        for copy in sums_y(g):
            copy.start()
        for j in range(GROUP):
            for r in range(2):
                at = slice(j * 192 + r * ROWS, j * 192 + r * ROWS + ROWS)
                ob[g, r, :, j * HD : (j + 1) * HD] = oh[g, at, :]
                dqb[g, r, :, j * HD : (j + 1) * HD] = dqh[g, at, :]
        copies, own = results(g)
        for copy in copies + own:
            copy.start()

    def sum_z(g):
        return remote(f"sumz{g}", rz_s.at[g], rz_r.at[g], anti)

    def reduce_y(g):
        for copy in sums_y(g):
            copy.wait_recv()

        def total(z):
            value = rs_s[g, y, z].astype(F32)
            for k in range(3):
                value = value + rs_r[g, k, z].astype(F32)
            return value

        rz_s[g] = total(zo).astype(BF16)
        sum_z(g).start()
        rz_o[g] = total(zh)

    def finals(g):
        copies, own = [], []
        place = pl.ds(pl.multiple_of(h * 256 + g * HD, HD), HD)
        for i, target in enumerate((ldk, ldv)):
            lanes = pl.ds(i * HD, HD)
            to = target.at[0, :, place]
            copies.append(remote(f"final{g}{i}", rfin.at[g, 1 - h, :, lanes], to, sib))
            own.append(
                pltpu.make_async_copy(rfin.at[g, h, :, lanes], to, loc.at[20 + 2 * g + i])
            )
        return copies, own

    def reduce_z(g):
        sum_z(g).wait_recv()
        rfin[g] = (rz_o[g] + rz_r[g].astype(F32)).astype(BF16)
        copies, own = finals(g)
        for copy in copies + own:
            copy.start()

    def tile(i, carry):
        g, t = i // TILES, i % TILES

        @pl.when(i == 0)
        def _():
            heads(0)

        @pl.when(i == FAR_AT)
        def _():
            pass_on(far_y(1), relays(1, zo, "f"))

        @pl.when(i == SECOND_AT)
        def _():
            begin_second()

        @pl.when(i == TILES)
        def _():
            give(0)
            heads(1)

        @pl.when(i == SUM_AT)
        def _():
            reduce_y(0)

        rows = pl.ds(pl.multiple_of(t * TILE, TILE), TILE)
        qt = qh[g, rows, :]
        ct = ch[g, rows, :]
        qp = qps[t % 3]
        s = dot_nt(kmat[...], qt)
        top = jnp.full((8, TILE), -1e30, F32)
        for b in range(KEYS // BLOCK):
            at = slice(b * BLOCK, (b + 1) * BLOCK)
            block = jnp.where(sub <= qp - bo[0, b] * BLOCK, s[at] * (SCALE * LOG2E), -1e30)
            sbuf[at, :] = block
            top = jnp.maximum(top, jnp.max(block.reshape(6, 8, TILE), axis=0))
        top = jnp.max(top, axis=0, keepdims=True)
        total = jnp.zeros((8, TILE), F32)
        for b in range(KEYS // BLOCK):
            at = slice(b * BLOCK, (b + 1) * BLOCK)
            block = jnp.exp2(sbuf[at, :] - top)
            sbuf[at, :] = block
            total = total + jnp.sum(block.reshape(6, 8, TILE), axis=0)
        inverse = 1.0 / jnp.sum(total, axis=0, keepdims=True)
        for b in range(KEYS // BLOCK):
            at = slice(b * BLOCK, (b + 1) * BLOCK)
            pbuf[at, :] = (sbuf[at, :] * inverse).astype(BF16)
        out = dot(vtr[...], pbuf[...])
        acc[:, HD:] += dot(pbuf[...], ct)
        oh[g, rows, :] = out.T.astype(BF16)
        delta = jnp.sum(out.astype(BF16).astype(F32) * ct.astype(F32).T, axis=0, keepdims=True)
        dprobs = dot_nt(vmat[...], ct)
        for b in range(KEYS // BLOCK):
            at = slice(b * BLOCK, (b + 1) * BLOCK)
            pbuf[at, :] = (sbuf[at, :] * ((dprobs[at] - delta) * inverse)).astype(BF16)
        dq = dot(ktr[...], pbuf[...])
        acc[:, :HD] += dot(pbuf[...], qt)
        dqh[g, rows, :] = (dq * SCALE).T.astype(BF16)
        return carry

    lax.fori_loop(0, 2 * TILES, tile, 0)
    give(1)
    for copy in second():
        copy.wait_recv()

    source = d ^ mask
    base = d - source + 2 * N_DP
    for a in range(4):
        for b in range(4):
            piece = r2[(base - (4 * a + b)) % N_DP]
            ks[b, 16 * a : 16 * a + 16, :] = piece[:, 1024:1152]
            vs[b, 16 * a : 16 * a + 16, :] = piece[:, 1152:1280]
            for j in range(GROUP):
                qs[b, j * SHORT + 16 * a : j * SHORT + 16 * a + 16, :] = piece[
                    :, j * HD : (j + 1) * HD
                ]
    width = GROUP * SHORT
    load_c.wait()
    for b in range(4):
        for j in range(GROUP):
            at = (b * GROUP + j) * HD
            cs[b, j * SHORT : (j + 1) * SHORT, :] = scb[:, at : at + HD]
    key_row = lax.broadcasted_iota(jnp.int32, (SHORT, width), 0)
    query_row = lax.broadcasted_iota(jnp.int32, (SHORT, width), 1) & (SHORT - 1)
    key_doc = jnp.zeros((SHORT, width), jnp.int32)
    query_doc = jnp.zeros((SHORT, width), jnp.int32)
    end = jnp.int32(0)
    for k in range(4):
        end = end + dl[0, k, source]
        key_doc = key_doc + jnp.where(key_row >= end, 1, 0)
        query_doc = query_doc + jnp.where(query_row >= end, 1, 0)
    allowed = (key_doc == query_doc) & (key_row <= query_row)
    for b in range(KV_HEADS):
        qt, ct, kt, vt = qs[b], cs[b], ks[b], vs[b]
        s = jnp.where(allowed, dot_nt(kt, qt) * (SCALE * LOG2E), -1e30)
        s = jnp.exp2(s - jnp.max(s, axis=0, keepdims=True))
        probs = s * (1.0 / jnp.sum(s, axis=0, keepdims=True))
        low = probs.astype(BF16)
        out = dot(vt.astype(F32).T.astype(BF16), low)
        sdv[0, :, b * HD : (b + 1) * HD] = dot(low, ct).astype(BF16)
        delta = jnp.sum(out.astype(BF16).astype(F32) * ct.astype(F32).T, axis=0, keepdims=True)
        ds = (probs * (dot_nt(vt, ct) - delta)).astype(BF16)
        dq = dot(kt.astype(F32).T.astype(BF16), ds) * SCALE
        sdk[0, :, b * HD : (b + 1) * HD] = (dot(ds, qt) * SCALE).astype(BF16)
        out = out.T.astype(BF16)
        dq = dq.T.astype(BF16)
        for j in range(GROUP):
            at = (b * GROUP + j) * HD
            so[0, :, at : at + HD] = out[j * SHORT : (j + 1) * SHORT]
            sdq[0, :, at : at + HD] = dq[j * SHORT : (j + 1) * SHORT]
    reduce_y(1)
    reduce_z(0)
    reduce_z(1)
    arrived, own = [], []
    for g in range(2):
        for copies, here in (results(g), finals(g)):
            arrived += copies
            own += here
    for copy in own:
        copy.wait()
    for copy in arrived:
        copy.wait_recv()
    for copy in waits + first() + second() + arrived:
        copy.wait_send()
    for g in range(2):
        late = relays(g, zh, "n") + relays(g, zo, "f") + far_y(g) + sums_y(g) + [sum_z(g)]
        for copy in late:
            copy.wait_send()


def write_out(*refs):
    sources, targets, held, sems = refs[:8], refs[8:16], refs[16:24], refs[24]
    first = [
        pltpu.make_async_copy(source, block, sems.at[i])
        for i, (source, block) in enumerate(zip(sources, held))
    ]
    second = [
        pltpu.make_async_copy(block, target, sems.at[8 + i])
        for i, (block, target) in enumerate(zip(held, targets))
    ]
    for copy in first:
        copy.start()
    for copy, after in zip(first, second):
        copy.wait()
        after.start()
    for copy in second:
        copy.wait()


def per_device(*args):
    any_spec = pl.BlockSpec(memory_space=pl.ANY)
    hbm = pl.BlockSpec(memory_space=pltpu.HBM)
    vmem = pl.BlockSpec(memory_space=pltpu.VMEM)
    smem = pl.BlockSpec(memory_space=pltpu.SMEM)
    dma = pltpu.SemaphoreType.DMA
    long_query, long_key, short_query, short_key = args[0], args[1], args[5], args[6]

    args = list(args)
    args[9] = jnp.transpose(args[9], (1, 2, 0))

    def shape(like):
        return jax.ShapeDtypeStruct(like.shape, like.dtype)

    def buffer(*dims, dtype=BF16):
        return pltpu.VMEM(dims, dtype)

    results = pl.pallas_call(
        kernel,
        out_shape=(
            shape(long_query), shape(long_query), shape(long_key), shape(long_key),
            shape(short_query), shape(short_query), shape(short_key), shape(short_key),
        ),
        in_specs=[hbm] * 4 + [smem] + [hbm] * 4 + [smem] * 2,
        out_specs=(any_spec,) * 4 + (vmem,) * 4,
        scratch_shapes=[
            buffer(ROWS, 512),
            buffer(ROWS, 512),
            buffer(SHORT, 4096),
            buffer(SHORT, 512),
            buffer(SHORT, 512),
            buffer(SHORT, 4096),
            buffer(2, 2, 4, 2, 2, ROWS, HD),
            buffer(2, 2, ROWS, HD),
            buffer(2, 2, ROWS, 1024),
            buffer(2, 2, ROWS, 1024),
            buffer(2, KEYS, HD),
            buffer(2, KEYS, HD),
            buffer(2, KEYS, HD),
            buffer(2, KEYS, HD),
            buffer(2, 2, ROWS, 1024),
            buffer(2, 2, ROWS, 1024),
            buffer(KEYS, HD),
            buffer(KEYS, HD),
            buffer(HD, KEYS),
            buffer(HD, KEYS),
            buffer(3, 1, TILE, dtype=jnp.int32),
            buffer(KEYS, TILE, dtype=F32),
            buffer(KEYS, TILE),
            buffer(KEYS, 256, dtype=F32),
            buffer(2, 4, 2, 2, ROWS, 256),
            buffer(2, 3, 2, 2, ROWS, 256),
            buffer(2, 2, ROWS, 256, dtype=F32),
            buffer(2, 2, ROWS, 256),
            buffer(2, 2, ROWS, 256),
            buffer(2, 2, ROWS, 256),
            buffer(N_DP, 16, 1280),
            buffer(N_DP, 16, 1280),
            buffer(N_DP, 16, 1280),
            buffer(N_DP, 16, 1280),
            buffer(4, GROUP * SHORT, HD),
            buffer(4, GROUP * SHORT, HD),
            buffer(4, SHORT, HD),
            buffer(4, SHORT, HD),
            dma((24,)), dma((SEMS,)), dma((SEMS,)),
        ],
        compiler_params=pltpu.CompilerParams(
            collective_id=0, has_side_effects=True, vmem_limit_bytes=VMEM_LIMIT
        ),
    )(*args)
    return pl.pallas_call(
        write_out,
        out_shape=tuple(shape(result) for result in results),
        in_specs=[any_spec] * 8,
        out_specs=(hbm,) * 8,
        scratch_shapes=[buffer(*result.shape) for result in results] + [dma((16,))],
        compiler_params=pltpu.CompilerParams(vmem_limit_bytes=VMEM_LIMIT),
    )(*results)


def solution(mesh):
    wide = P("dp", "ctx", None)
    return jax.shard_map(
        per_device,
        mesh=mesh,
        in_specs=(wide,) * 4
        + (P("dp", None),)
        + (wide,) * 4
        + (P(None, "ctx", None), P("ctx", None)),
        out_specs=(wide,) * 8,
        check_vma=False,
    )
```

```python
import jax
import jax.numpy as jnp
from jax import lax
from jax.experimental import pallas as pl
from jax.experimental.pallas import tpu as pltpu
from jax.sharding import PartitionSpec as P

HD = 128
GROUP = 8
KV_HEADS = 4
ROWS = 96
BLOCK = 48
KEYS = 1536
SHORT = 64
TILE = 256
TILES = KEYS // TILE
N_DP = 16
SEMS = 256
VMEM_LIMIT = 62 * 1024 * 1024
PIPE = 3
CHUNK = 384
SCALE = HD**-0.5
LOG2E = 1.4426950408889634
NT = (((1,), (1,)), ((), ()))
F32 = jnp.float32
BF16 = jnp.bfloat16
MESH = pl.DeviceIdType.MESH


def dot(a, b):
    return jnp.dot(a, b, preferred_element_type=F32)


def dot_nt(a, b):
    return lax.dot_general(a, b, NT, preferred_element_type=F32)


def kernel(
    lq, lk, lv, lc, bo, sq, sk, sv, sc, dl, bl,
    lo, ldq, ldk, ldv, so, sdq, sdk, sdv,
    lkb, lvb, sqb, skb, svb, scb,
    kv, kvx, qb, cb, qh, ch, oh, dqh, ob, dqb, kmat, vmat, ktr, vtr, qps, sbuf, pbuf, dbuf, delta,
    rs_s, rs_r, rz_o, rz_s, rz_r, rfin,
    st, r1, s2, r2, qs, cs, ks, vs,
    loc, sends, recvs,
):
    d = lax.axis_index("dp")
    c = lax.axis_index("ctx")
    h = c % 2
    y = (c // 2) % 4
    zh = c // 8
    zo = 1 - zh
    ylow, yhigh = (y + 3) % 4, (y + 1) % 4
    sib = {"ctx": c + 1 - 2 * h}
    anti = {"ctx": (c + 8) % 16}
    mask = bl[0, 0]

    def at_y(k):
        return {"ctx": zh * 8 + ((y + k) % 4) * 2 + h}

    def at_dp(k):
        return {"dp": (d + k) % N_DP}

    numbers = {}

    def remote(name, src, dst, to, extra=0):
        number = numbers.setdefault(name, 3 * len(numbers)) + extra
        return pltpu.make_async_remote_copy(
            src_ref=src,
            dst_ref=dst,
            send_sem=sends.at[number],
            recv_sem=recvs.at[number],
            device_id=to,
            device_id_type=MESH,
        )

    barrier = pltpu.get_barrier_semaphore()
    peers = [sib, anti] + [at_y(k) for k in range(1, 4)] + [at_dp(k) for k in range(1, N_DP)]
    for peer in peers:
        pl.semaphore_signal(barrier, inc=1, device_id=peer, device_id_type=MESH)

    local = []

    def load(src, dst):
        copy = pltpu.make_async_copy(src, dst, loc.at[len(local)])
        copy.start()
        local.append(copy)
        return copy

    load_k, load_v = load(lk.at[0], lkb), load(lv.at[0], lvb)
    load_s = [load(sq.at[0], sqb), load(sk.at[0], skb), load(sv.at[0], svb)]

    def wide(core, g):
        return pl.ds(pl.multiple_of(core * 2048 + g * 1024, 1024), 1024)

    own_rows = [
        [load(lq.at[0, :, wide(h, g)], qb.at[g, h]), load(lc.at[0, :, wide(h, g)], cb.at[g, h])]
        for g in range(2)
    ]
    load_c = load(sc.at[0], scb)

    for part in range(3):
        column = lax.broadcasted_iota(jnp.int32, (1, TILE), 1) + part * TILE
        position = jnp.zeros((1, TILE), jnp.int32)
        for k in range(16):
            start = bo[0, zh * 16 + y * 4 + k % 4] * BLOCK - BLOCK * k
            position = jnp.where(column >= BLOCK * k, column + start, position)
        qps[part] = position

    load_k.wait()
    load_v.wait()
    for g in range(2):
        mine = pl.ds(pl.multiple_of(h * 256 + g * HD, HD), HD)
        other = pl.ds(pl.multiple_of((1 - h) * 256 + g * HD, HD), HD)
        kv[g, zh, y, h, 0] = lkb[:, mine]
        kv[g, zh, y, h, 1] = lvb[:, mine]
        kvx[g, 0] = lkb[:, other]
        kvx[g, 1] = lvb[:, other]

    for copy in load_s:
        copy.wait()
    for a in range(4):
        for b in range(4):
            rows = slice(16 * a, 16 * a + 16)
            st[4 * a + b, :, 0:1024] = sqb[rows, 1024 * b : 1024 * b + 1024]
            st[4 * a + b, :, 1024:1152] = skb[rows, 128 * b : 128 * b + 128]
            st[4 * a + b, :, 1152:1280] = svb[rows, 128 * b : 128 * b + 128]
    r1[0] = st[0]

    pl.semaphore_wait(barrier, len(peers))

    waits = []

    def begin(copy):
        copy.start()
        waits.append(copy)
        return copy

    def same(name, block, to):
        return remote(name, block, block, to)

    sib_kv = [
        begin(remote(f"sib{g}", kvx.at[g], kv.at[g, zh, y, h], sib)) for g in range(2)
    ]
    def far(g, core, name):
        return same(f"z{g}{name}", kv.at[g, zh, y, core], anti)

    def near_y(g):
        return [
            begin(same(f"up{g}", kv.at[g, zh, y], at_y(1))),
            begin(same(f"down{g}", kv.at[g, zh, y], at_y(3))),
        ]

    z0 = [begin(far(0, h, "own"))]
    sib_kv[0].wait_recv()
    z0.append(begin(far(0, 1 - h, "sib")))
    own_y = [near_y(0)]
    sib_rows = [
        [
            begin(remote(f"q{k}", lq.at[0, :, wide(1 - h, k)], qb.at[k, h], sib)),
            begin(remote(f"c{k}", lc.at[0, :, wide(1 - h, k)], cb.at[k, h], sib)),
        ]
        for k in range(2)
    ]
    sib_kv[1].wait_recv()
    z1 = [begin(far(1, h, "own")), begin(far(1, 1 - h, "sib"))]
    own_y.append(near_y(1))

    def first():
        return [remote(f"first{p}", st.at[p], r1.at[p], at_dp(p)) for p in range(1, N_DP)]

    def second():
        return [remote(f"second{p}", s2.at[p], r2.at[p], at_dp(p)) for p in range(1, N_DP)]

    def begin_first():
        for copy in first():
            copy.start()

    def begin_second():
        for copy in first():
            copy.wait_recv()
        for k in range(N_DP):
            s2[k] = r1[(d - ((d + k) % N_DP ^ mask) + N_DP) % N_DP]
        r2[0] = s2[0]
        for copy in second():
            copy.start()

    def arrange(g):
        for copy in own_rows[g]:
            copy.wait()
        for copy in sib_rows[g]:
            copy.wait_recv()
        for j in range(GROUP):
            for r in range(2):
                to = slice(j * 192 + r * ROWS, j * 192 + r * ROWS + ROWS)
                at = slice(j * HD, (j + 1) * HD)
                qh[g, to, :] = qb[g, r, :, at]
                ch[g, to, :] = cb[g, r, :, at]

    def relays(g, z, name):
        return [
            same(f"relay{g}{name}0", kv.at[g, z, ylow, 0], at_y(1)),
            same(f"relay{g}{name}1", kv.at[g, z, yhigh, 1], at_y(3)),
        ]

    def far_y(g):
        return [
            same(f"upfar{g}", kv.at[g, zo, y], at_y(1)),
            same(f"downfar{g}", kv.at[g, zo, y], at_y(3)),
        ]

    def pass_on(arrived, onward):
        for copy, after in zip(arrived, onward):
            copy.wait_recv()
            after.start()

    arrange(0)
    pass_on(own_y[0], relays(0, zh, "n"))
    for copy in z0:
        copy.wait_recv()
    for copy in far_y(0):
        copy.start()
    begin_first()
    pass_on(own_y[1], relays(1, zh, "n"))
    arrange(1)
    pass_on(far_y(0), relays(0, zo, "f"))

    sub = lax.broadcasted_iota(jnp.int32, (BLOCK, TILE), 0)

    def heads(g):
        for copy in relays(g, zh, "n") + relays(g, zo, "f"):
            copy.wait_recv()
        for z in range(2):
            for row in range(4):
                to = slice(row * CHUNK + z * 192, row * CHUNK + z * 192 + 192)
                kmat[to, :] = kv[g, z, row, :, 0].reshape(192, HD)
                vmat[to, :] = kv[g, z, row, :, 1].reshape(192, HD)
        ktr[...] = kmat[...].T
        vtr[...] = vmat[...].T

    def sum_y(g, k):
        source = rs_s.at[g, (y + 1 + k) % 4]
        return remote(f"sum{g}", source, rs_r.at[g, k], at_y(k + 1), k)

    def sums_y(g):
        return [sum_y(g, k) for k in range(3)]

    def results(g):
        copies, own = [], []
        for i, (source, target) in enumerate(((ob, lo), (dqb, ldq))):
            place = target.at[0, :, wide(h, g)]
            copies.append(remote(f"out{g}{i}", source.at[g, 1 - h], place, sib))
            own.append(pltpu.make_async_copy(source.at[g, h], place, loc.at[16 + 2 * g + i]))
        return copies, own

    def give(g):
        for j in range(GROUP):
            for r in range(2):
                at = slice(j * 192 + r * ROWS, j * 192 + r * ROWS + ROWS)
                ob[g, r, :, j * HD : (j + 1) * HD] = oh[g, at, :]
                dqb[g, r, :, j * HD : (j + 1) * HD] = dqh[g, at, :]
        copies, own = results(g)
        for copy in copies + own:
            copy.start()

    def sum_z(g):
        return remote(f"sumz{g}", rz_s.at[g], rz_r.at[g], anti)

    def reduce_y(g):
        for copy in sums_y(g):
            copy.wait_recv()

        def total(z):
            value = rs_s[g, y, z].astype(F32)
            for k in range(3):
                value = value + rs_r[g, k, z].astype(F32)
            return value

        rz_s[g] = total(zo).astype(BF16)
        sum_z(g).start()
        rz_o[g] = total(zh)

    def finals(g):
        copies, own = [], []
        place = pl.ds(pl.multiple_of(h * 256 + g * HD, HD), HD)
        for i, target in enumerate((ldk, ldv)):
            lanes = pl.ds(i * HD, HD)
            to = target.at[0, :, place]
            copies.append(remote(f"final{g}{i}", rfin.at[g, 1 - h, :, lanes], to, sib))
            own.append(
                pltpu.make_async_copy(rfin.at[g, h, :, lanes], to, loc.at[20 + 2 * g + i])
            )
        return copies, own

    def reduce_z(g):
        sum_z(g).wait_recv()
        rfin[g] = (rz_o[g] + rz_r[g].astype(F32)).astype(BF16)
        copies, own = finals(g)
        for copy in copies + own:
            copy.start()

    def forward(g, between):
        def steps(t, slot):
            rows = pl.ds(pl.multiple_of(t * TILE, TILE), TILE)
            lanes = slice(slot * TILE, (slot + 1) * TILE)
            held = {}

            def scores():
                s = dot_nt(kmat[...], qh[g, rows, :])
                top = jnp.full((8, TILE), -1e30, F32)
                for b in range(KEYS // BLOCK):
                    at = slice(b * BLOCK, (b + 1) * BLOCK)
                    place = (b % 8) // 4 * 16 + b // 8 * 4 + b % 4
                    seen = sub <= qps[slot] - bo[0, place] * BLOCK
                    block = jnp.where(seen, s[at] * (SCALE * LOG2E), -1e30)
                    sbuf[at, lanes] = block
                    top = jnp.maximum(top, jnp.max(block.reshape(6, 8, TILE), axis=0))
                held["top"] = jnp.max(top, axis=0, keepdims=True)

            def exps():
                total = jnp.zeros((8, TILE), F32)
                for b in range(KEYS // BLOCK):
                    at = slice(b * BLOCK, (b + 1) * BLOCK)
                    block = jnp.exp2(sbuf[at, lanes] - held["top"])
                    pbuf[at, rows] = block.astype(BF16)
                    total = total + jnp.sum(block.reshape(6, 8, TILE), axis=0)
                held["inverse"] = 1.0 / jnp.sum(total, axis=0, keepdims=True)

            def outputs():
                inverse = held["inverse"]
                out = dot(vtr[...], pbuf[:, rows]) * inverse
                oh[g, rows, :] = out.T.astype(BF16)
                cot = ch[g, rows, :].astype(F32).T
                low = out.astype(BF16).astype(F32)
                delta[t] = jnp.sum(low * cot, axis=0, keepdims=True) * inverse
                ch[g, rows, :] = (cot * inverse).T.astype(BF16)

            return scores, exps, outputs

        def body(i, carry):
            @pl.when(i == 1)
            def _():
                between()

            parts = [steps(i * PIPE + k, k) for k in range(PIPE)]
            for step in range(PIPE + 2):
                for stage in (2, 1, 0):
                    if 0 <= step - stage < PIPE:
                        parts[step - stage][stage]()
            return carry

        lax.fori_loop(0, TILES // PIPE, body, 0)

    def backward(g):
        def body(k, carry):
            row = (y + 1 + k) % 4
            keys = pl.ds(pl.multiple_of(row * CHUNK, CHUNK), CHUNK)
            values = vmat[keys, :]
            for t in range(TILES):
                cols = slice(t * TILE, (t + 1) * TILE)
                dprobs = dot_nt(values, ch[g, cols, :])
                dscores = pbuf[keys, cols].astype(F32) * (dprobs - delta[t])
                dbuf[keys, cols] = dscores.astype(BF16)
            value_grad = dot(pbuf[keys, :], ch[g])
            key_grad = dot(dbuf[keys, :], qh[g]) * SCALE
            rs_s[g, row, :, :, :, HD:] = value_grad.astype(BF16).reshape(2, 2, ROWS, HD)
            rs_s[g, row, :, :, :, :HD] = key_grad.astype(BF16).reshape(2, 2, ROWS, HD)

            @pl.when(k < 3)
            def _():
                sum_y(g, k).start()

            return carry

        lax.fori_loop(0, 4, body, 0)

    def query_grads(g):
        for t in range(2):
            cols = slice(t * 768, (t + 1) * 768)
            dqh[g, cols, :] = (dot(ktr[...], dbuf[:, cols]) * SCALE).T.astype(BF16)

    def pass_far():
        pass_on(far_y(1), relays(1, zo, "f"))

    for copy in z1:
        copy.wait_recv()
    for copy in far_y(1):
        copy.start()
    heads(0)
    forward(0, pass_far)
    backward(0)
    begin_second()
    query_grads(0)
    give(0)
    heads(1)
    forward(1, lambda: None)
    reduce_y(0)
    backward(1)
    query_grads(1)
    give(1)
    reduce_z(0)
    reduce_y(1)
    for copy in second():
        copy.wait_recv()

    source = d ^ mask
    base = d - source + 2 * N_DP
    for a in range(4):
        for b in range(4):
            piece = r2[(base - (4 * a + b)) % N_DP]
            ks[b, 16 * a : 16 * a + 16, :] = piece[:, 1024:1152]
            vs[b, 16 * a : 16 * a + 16, :] = piece[:, 1152:1280]
            for j in range(GROUP):
                qs[b, j * SHORT + 16 * a : j * SHORT + 16 * a + 16, :] = piece[
                    :, j * HD : (j + 1) * HD
                ]
    width = GROUP * SHORT
    load_c.wait()
    for b in range(4):
        for j in range(GROUP):
            at = (b * GROUP + j) * HD
            cs[b, j * SHORT : (j + 1) * SHORT, :] = scb[:, at : at + HD]
    key_row = lax.broadcasted_iota(jnp.int32, (SHORT, width), 0)
    query_row = lax.broadcasted_iota(jnp.int32, (SHORT, width), 1) & (SHORT - 1)
    key_doc = jnp.zeros((SHORT, width), jnp.int32)
    query_doc = jnp.zeros((SHORT, width), jnp.int32)
    end = jnp.int32(0)
    for k in range(4):
        end = end + dl[0, k, source]
        key_doc = key_doc + jnp.where(key_row >= end, 1, 0)
        query_doc = query_doc + jnp.where(query_row >= end, 1, 0)
    allowed = (key_doc == query_doc) & (key_row <= query_row)
    for b in range(KV_HEADS):
        qt, ct, kt, vt = qs[b], cs[b], ks[b], vs[b]
        s = jnp.where(allowed, dot_nt(kt, qt) * (SCALE * LOG2E), -1e30)
        s = jnp.exp2(s - jnp.max(s, axis=0, keepdims=True))
        probs = s * (1.0 / jnp.sum(s, axis=0, keepdims=True))
        low = probs.astype(BF16)
        out = dot(vt.astype(F32).T.astype(BF16), low)
        sdv[0, :, b * HD : (b + 1) * HD] = dot(low, ct).astype(BF16)
        sums = jnp.sum(out.astype(BF16).astype(F32) * ct.astype(F32).T, axis=0, keepdims=True)
        ds = (probs * (dot_nt(vt, ct) - sums)).astype(BF16)
        dq = dot(kt.astype(F32).T.astype(BF16), ds) * SCALE
        sdk[0, :, b * HD : (b + 1) * HD] = (dot(ds, qt) * SCALE).astype(BF16)
        out = out.T.astype(BF16)
        dq = dq.T.astype(BF16)
        for j in range(GROUP):
            at = (b * GROUP + j) * HD
            so[0, :, at : at + HD] = out[j * SHORT : (j + 1) * SHORT]
            sdq[0, :, at : at + HD] = dq[j * SHORT : (j + 1) * SHORT]
    reduce_z(1)
    arrived, own = [], []
    for g in range(2):
        for copies, here in (results(g), finals(g)):
            arrived += copies
            own += here
    for copy in own:
        copy.wait()
    for copy in arrived:
        copy.wait_recv()
    for copy in waits + first() + second() + arrived:
        copy.wait_send()
    for g in range(2):
        late = relays(g, zh, "n") + relays(g, zo, "f") + far_y(g) + sums_y(g) + [sum_z(g)]
        for copy in late:
            copy.wait_send()


def write_out(*refs):
    sources, targets, held, sems = refs[:8], refs[8:16], refs[16:24], refs[24]
    first = [
        pltpu.make_async_copy(source, block, sems.at[i])
        for i, (source, block) in enumerate(zip(sources, held))
    ]
    second = [
        pltpu.make_async_copy(block, target, sems.at[8 + i])
        for i, (block, target) in enumerate(zip(held, targets))
    ]
    for copy in first:
        copy.start()
    for copy, after in zip(first, second):
        copy.wait()
        after.start()
    for copy in second:
        copy.wait()


def per_device(*args):
    any_spec = pl.BlockSpec(memory_space=pl.ANY)
    hbm = pl.BlockSpec(memory_space=pltpu.HBM)
    vmem = pl.BlockSpec(memory_space=pltpu.VMEM)
    smem = pl.BlockSpec(memory_space=pltpu.SMEM)
    dma = pltpu.SemaphoreType.DMA
    long_query, long_key, short_query, short_key = args[0], args[1], args[5], args[6]

    args = list(args)
    args[9] = jnp.transpose(args[9], (1, 2, 0))

    def shape(like):
        return jax.ShapeDtypeStruct(like.shape, like.dtype)

    def buffer(*dims, dtype=BF16):
        return pltpu.VMEM(dims, dtype)

    results = pl.pallas_call(
        kernel,
        out_shape=(
            shape(long_query), shape(long_query), shape(long_key), shape(long_key),
            shape(short_query), shape(short_query), shape(short_key), shape(short_key),
        ),
        in_specs=[hbm] * 4 + [smem] + [hbm] * 4 + [smem] * 2,
        out_specs=(any_spec,) * 4 + (vmem,) * 4,
        scratch_shapes=[
            buffer(ROWS, 512),
            buffer(ROWS, 512),
            buffer(SHORT, 4096),
            buffer(SHORT, 512),
            buffer(SHORT, 512),
            buffer(SHORT, 4096),
            buffer(2, 2, 4, 2, 2, ROWS, HD),
            buffer(2, 2, ROWS, HD),
            buffer(2, 2, ROWS, 1024),
            buffer(2, 2, ROWS, 1024),
            buffer(2, KEYS, HD),
            buffer(2, KEYS, HD),
            buffer(2, KEYS, HD),
            buffer(2, KEYS, HD),
            buffer(2, 2, ROWS, 1024),
            buffer(2, 2, ROWS, 1024),
            buffer(KEYS, HD),
            buffer(KEYS, HD),
            buffer(HD, KEYS),
            buffer(HD, KEYS),
            buffer(3, 1, TILE, dtype=jnp.int32),
            buffer(KEYS, PIPE * TILE, dtype=F32),
            buffer(KEYS, KEYS),
            buffer(KEYS, KEYS),
            buffer(TILES, 1, TILE, dtype=F32),
            buffer(2, 4, 2, 2, ROWS, 256),
            buffer(2, 3, 2, 2, ROWS, 256),
            buffer(2, 2, ROWS, 256, dtype=F32),
            buffer(2, 2, ROWS, 256),
            buffer(2, 2, ROWS, 256),
            buffer(2, 2, ROWS, 256),
            buffer(N_DP, 16, 1280),
            buffer(N_DP, 16, 1280),
            buffer(N_DP, 16, 1280),
            buffer(N_DP, 16, 1280),
            buffer(4, GROUP * SHORT, HD),
            buffer(4, GROUP * SHORT, HD),
            buffer(4, SHORT, HD),
            buffer(4, SHORT, HD),
            dma((24,)), dma((SEMS,)), dma((SEMS,)),
        ],
        compiler_params=pltpu.CompilerParams(
            collective_id=0, has_side_effects=True, vmem_limit_bytes=VMEM_LIMIT
        ),
    )(*args)
    return pl.pallas_call(
        write_out,
        out_shape=tuple(shape(result) for result in results),
        in_specs=[any_spec] * 8,
        out_specs=(hbm,) * 8,
        scratch_shapes=[buffer(*result.shape) for result in results] + [dma((16,))],
        compiler_params=pltpu.CompilerParams(vmem_limit_bytes=VMEM_LIMIT),
    )(*results)


def solution(mesh):
    wide = P("dp", "ctx", None)
    return jax.shard_map(
        per_device,
        mesh=mesh,
        in_specs=(wide,) * 4
        + (P("dp", None),)
        + (wide,) * 4
        + (P(None, "ctx", None), P("ctx", None)),
        out_specs=(wide,) * 8,
        check_vma=False,
    )
```

```python
import jax
import jax.numpy as jnp
from jax import lax
from jax.experimental import pallas as pl
from jax.experimental.pallas import tpu as pltpu
from jax.sharding import PartitionSpec as P

HD = 128
GROUP = 8
KV_HEADS = 4
ROWS = 96
BLOCK = 48
KEYS = 1536
SHORT = 64
TILE = 256
TILES = KEYS // TILE
N_DP = 16
SEMS = 256
VMEM_LIMIT = 62 * 1024 * 1024
PIPE = 3
CHUNK = 384
SCALE = HD**-0.5
LOG2E = 1.4426950408889634
NT = (((1,), (1,)), ((), ()))
F32 = jnp.float32
BF16 = jnp.bfloat16
MESH = pl.DeviceIdType.MESH


def dot(a, b):
    return jnp.dot(a, b, preferred_element_type=F32)


def dot_nt(a, b):
    return lax.dot_general(a, b, NT, preferred_element_type=F32)


def kernel(
    lq, lk, lv, lc, bo, sq, sk, sv, sc, dl, bl,
    lo, ldq, ldk, ldv, so, sdq, sdk, sdv,
    lkb, lvb, sqb, skb, svb, scb,
    kv, kvx, qb, cb, qh, ch, oh, dqh, ob, dqb, kmat, vmat, ktr, vtr, qps, sbuf, pbuf, dbuf, delta,
    rs_s, rs_r, rz_o, rz_s, rz_r, rfin,
    st, r1, s2, r2, qs, cs, ks, vs, sob, sdqb, sdkb, sdvb,
    loc, sends, recvs,
):
    d = lax.axis_index("dp")
    c = lax.axis_index("ctx")
    h = c % 2
    y = (c // 2) % 4
    zh = c // 8
    zo = 1 - zh
    ylow, yhigh = (y + 3) % 4, (y + 1) % 4
    sib = {"ctx": c + 1 - 2 * h}
    anti = {"ctx": (c + 8) % 16}
    mask = bl[0, 0]

    def at_y(k):
        return {"ctx": zh * 8 + ((y + k) % 4) * 2 + h}

    def at_dp(k):
        return {"dp": (d + k) % N_DP}

    numbers = {}

    def remote(name, src, dst, to, extra=0):
        number = numbers.setdefault(name, 3 * len(numbers)) + extra
        return pltpu.make_async_remote_copy(
            src_ref=src,
            dst_ref=dst,
            send_sem=sends.at[number],
            recv_sem=recvs.at[number],
            device_id=to,
            device_id_type=MESH,
        )

    barrier = pltpu.get_barrier_semaphore()
    peers = [sib, anti] + [at_y(k) for k in range(1, 4)] + [at_dp(k) for k in range(1, N_DP)]
    for peer in peers:
        pl.semaphore_signal(barrier, inc=1, device_id=peer, device_id_type=MESH)

    local = []

    def load(src, dst):
        copy = pltpu.make_async_copy(src, dst, loc.at[len(local)])
        copy.start()
        local.append(copy)
        return copy

    load_k, load_v = load(lk.at[0], lkb), load(lv.at[0], lvb)
    load_s = [load(sq.at[0], sqb), load(sk.at[0], skb), load(sv.at[0], svb)]

    def wide(core, g):
        return pl.ds(pl.multiple_of(core * 2048 + g * 1024, 1024), 1024)

    own_rows = [
        [load(lq.at[0, :, wide(h, g)], qb.at[g, h]), load(lc.at[0, :, wide(h, g)], cb.at[g, h])]
        for g in range(2)
    ]
    load_c = load(sc.at[0], scb)

    for part in range(3):
        column = lax.broadcasted_iota(jnp.int32, (1, TILE), 1) + part * TILE
        position = jnp.zeros((1, TILE), jnp.int32)
        for k in range(16):
            start = bo[0, zh * 16 + y * 4 + k % 4] * BLOCK - BLOCK * k
            position = jnp.where(column >= BLOCK * k, column + start, position)
        qps[part] = position

    load_k.wait()
    load_v.wait()
    for g in range(2):
        mine = pl.ds(pl.multiple_of(h * 256 + g * HD, HD), HD)
        other = pl.ds(pl.multiple_of((1 - h) * 256 + g * HD, HD), HD)
        kv[g, zh, y, h, 0] = lkb[:, mine]
        kv[g, zh, y, h, 1] = lvb[:, mine]
        kvx[g, 0] = lkb[:, other]
        kvx[g, 1] = lvb[:, other]

    for copy in load_s:
        copy.wait()
    for a in range(4):
        for b in range(4):
            rows = slice(16 * a, 16 * a + 16)
            st[4 * a + b, :, 0:1024] = sqb[rows, 1024 * b : 1024 * b + 1024]
            st[4 * a + b, :, 1024:1152] = skb[rows, 128 * b : 128 * b + 128]
            st[4 * a + b, :, 1152:1280] = svb[rows, 128 * b : 128 * b + 128]
    r1[0] = st[0]

    pl.semaphore_wait(barrier, len(peers))

    waits = []

    def begin(copy):
        copy.start()
        waits.append(copy)
        return copy

    def same(name, block, to):
        return remote(name, block, block, to)

    sib_kv = [
        begin(remote(f"sib{g}", kvx.at[g], kv.at[g, zh, y, h], sib)) for g in range(2)
    ]
    def far(g, core, name):
        return same(f"z{g}{name}", kv.at[g, zh, y, core], anti)

    def near_y(g):
        return [
            begin(same(f"up{g}", kv.at[g, zh, y], at_y(1))),
            begin(same(f"down{g}", kv.at[g, zh, y], at_y(3))),
        ]

    z0 = [begin(far(0, h, "own"))]
    sib_kv[0].wait_recv()
    z0.append(begin(far(0, 1 - h, "sib")))
    own_y = [near_y(0)]
    sib_rows = [
        [
            begin(remote(f"q{k}", lq.at[0, :, wide(1 - h, k)], qb.at[k, h], sib)),
            begin(remote(f"c{k}", lc.at[0, :, wide(1 - h, k)], cb.at[k, h], sib)),
        ]
        for k in range(2)
    ]
    sib_kv[1].wait_recv()
    z1 = [begin(far(1, h, "own")), begin(far(1, 1 - h, "sib"))]
    own_y.append(near_y(1))

    def first():
        return [remote(f"first{p}", st.at[p], r1.at[p], at_dp(p)) for p in range(1, N_DP)]

    def second():
        return [remote(f"second{p}", s2.at[p], r2.at[p], at_dp(p)) for p in range(1, N_DP)]

    def begin_first():
        for copy in first():
            copy.start()

    def begin_second():
        for copy in first():
            copy.wait_recv()
        for k in range(N_DP):
            s2[k] = r1[(d - ((d + k) % N_DP ^ mask) + N_DP) % N_DP]
        r2[0] = s2[0]
        for copy in second():
            copy.start()

    def arrange(g):
        for copy in own_rows[g]:
            copy.wait()
        for copy in sib_rows[g]:
            copy.wait_recv()
        for j in range(GROUP):
            for r in range(2):
                to = slice(j * 192 + r * ROWS, j * 192 + r * ROWS + ROWS)
                at = slice(j * HD, (j + 1) * HD)
                qh[g, to, :] = qb[g, r, :, at]
                ch[g, to, :] = cb[g, r, :, at]

    def relays(g, z, name):
        return [
            same(f"relay{g}{name}0", kv.at[g, z, ylow, 0], at_y(1)),
            same(f"relay{g}{name}1", kv.at[g, z, yhigh, 1], at_y(3)),
        ]

    def far_y(g):
        return [
            same(f"upfar{g}", kv.at[g, zo, y], at_y(1)),
            same(f"downfar{g}", kv.at[g, zo, y], at_y(3)),
        ]

    def pass_on(arrived, onward):
        for copy, after in zip(arrived, onward):
            copy.wait_recv()
            after.start()

    arrange(0)
    pass_on(own_y[0], relays(0, zh, "n"))
    for copy in z0:
        copy.wait_recv()
    for copy in far_y(0):
        copy.start()
    begin_first()
    pass_on(own_y[1], relays(1, zh, "n"))
    arrange(1)
    pass_on(far_y(0), relays(0, zo, "f"))

    sub = lax.broadcasted_iota(jnp.int32, (BLOCK, TILE), 0)

    def heads(g):
        for copy in relays(g, zh, "n") + relays(g, zo, "f"):
            copy.wait_recv()
        for z in range(2):
            for row in range(4):
                to = slice(row * CHUNK + z * 192, row * CHUNK + z * 192 + 192)
                kmat[to, :] = kv[g, z, row, :, 0].reshape(192, HD)
                vmat[to, :] = kv[g, z, row, :, 1].reshape(192, HD)
        ktr[...] = kmat[...].T
        vtr[...] = vmat[...].T

    def sum_y(g, k):
        source = rs_s.at[g, (y + 1 + k) % 4]
        return remote(f"sum{g}", source, rs_r.at[g, k], at_y(k + 1), k)

    def sums_y(g):
        return [sum_y(g, k) for k in range(3)]

    def results(g):
        copies, own = [], []
        for i, (source, target) in enumerate(((ob, lo), (dqb, ldq))):
            place = target.at[0, :, wide(h, g)]
            copies.append(remote(f"out{g}{i}", source.at[g, 1 - h], place, sib))
            own.append(pltpu.make_async_copy(source.at[g, h], place, loc.at[16 + 2 * g + i]))
        return copies, own

    def give(g):
        for j in range(GROUP):
            for r in range(2):
                at = slice(j * 192 + r * ROWS, j * 192 + r * ROWS + ROWS)
                ob[g, r, :, j * HD : (j + 1) * HD] = oh[g, at, :]
                dqb[g, r, :, j * HD : (j + 1) * HD] = dqh[g, at, :]
        copies, own = results(g)
        for copy in copies + own:
            copy.start()

    def sum_z(g):
        return remote(f"sumz{g}", rz_s.at[g], rz_r.at[g], anti)

    def reduce_y(g):
        for copy in sums_y(g):
            copy.wait_recv()

        def total(z):
            value = rs_s[g, y, z].astype(F32)
            for k in range(3):
                value = value + rs_r[g, k, z].astype(F32)
            return value

        rz_s[g] = total(zo).astype(BF16)
        sum_z(g).start()
        rz_o[g] = total(zh)

    def finals(g):
        copies, own = [], []
        place = pl.ds(pl.multiple_of(h * 256 + g * HD, HD), HD)
        for i, target in enumerate((ldk, ldv)):
            lanes = pl.ds(i * HD, HD)
            to = target.at[0, :, place]
            copies.append(remote(f"final{g}{i}", rfin.at[g, 1 - h, :, lanes], to, sib))
            own.append(
                pltpu.make_async_copy(rfin.at[g, h, :, lanes], to, loc.at[20 + 2 * g + i])
            )
        return copies, own

    def reduce_z(g):
        sum_z(g).wait_recv()
        rfin[g] = (rz_o[g] + rz_r[g].astype(F32)).astype(BF16)
        copies, own = finals(g)
        for copy in copies + own:
            copy.start()

    def forward(g, between):
        def steps(t, slot):
            rows = pl.ds(pl.multiple_of(t * TILE, TILE), TILE)
            lanes = slice(slot * TILE, (slot + 1) * TILE)
            held = {}

            def scores():
                s = dot_nt(kmat[...], qh[g, rows, :])
                top = jnp.full((8, TILE), -1e30, F32)
                for b in range(KEYS // BLOCK):
                    at = slice(b * BLOCK, (b + 1) * BLOCK)
                    place = (b % 8) // 4 * 16 + b // 8 * 4 + b % 4
                    seen = sub <= qps[slot] - bo[0, place] * BLOCK
                    block = jnp.where(seen, s[at] * (SCALE * LOG2E), -1e30)
                    sbuf[at, lanes] = block
                    top = jnp.maximum(top, jnp.max(block.reshape(6, 8, TILE), axis=0))
                held["top"] = jnp.max(top, axis=0, keepdims=True)

            def exps():
                total = jnp.zeros((8, TILE), F32)
                for b in range(KEYS // BLOCK):
                    at = slice(b * BLOCK, (b + 1) * BLOCK)
                    block = jnp.exp2(sbuf[at, lanes] - held["top"])
                    pbuf[at, rows] = block.astype(BF16)
                    total = total + jnp.sum(block.reshape(6, 8, TILE), axis=0)
                held["inverse"] = 1.0 / jnp.sum(total, axis=0, keepdims=True)

            def outputs():
                inverse = held["inverse"]
                out = dot(vtr[...], pbuf[:, rows]) * inverse
                oh[g, rows, :] = out.T.astype(BF16)
                cot = ch[g, rows, :].astype(F32).T
                low = out.astype(BF16).astype(F32)
                delta[t] = jnp.sum(low * cot, axis=0, keepdims=True) * inverse
                ch[g, rows, :] = (cot * inverse).T.astype(BF16)

            return scores, exps, outputs

        def body(i, carry):
            @pl.when(i == 1)
            def _():
                between()

            parts = [steps(i * PIPE + k, k) for k in range(PIPE)]
            for step in range(PIPE + 2):
                for stage in (2, 1, 0):
                    if 0 <= step - stage < PIPE:
                        parts[step - stage][stage]()
            return carry

        lax.fori_loop(0, TILES // PIPE, body, 0)

    def backward(g):
        def body(k, carry):
            row = (y + 1 + k) % 4
            keys = pl.ds(pl.multiple_of(row * CHUNK, CHUNK), CHUNK)
            values = vmat[keys, :]
            for t in range(TILES):
                cols = slice(t * TILE, (t + 1) * TILE)
                dprobs = dot_nt(values, ch[g, cols, :])
                dscores = pbuf[keys, cols].astype(F32) * (dprobs - delta[t])
                dbuf[keys, cols] = dscores.astype(BF16)
            value_grad = dot(pbuf[keys, :], ch[g])
            key_grad = dot(dbuf[keys, :], qh[g]) * SCALE
            rs_s[g, row, :, :, :, HD:] = value_grad.astype(BF16).reshape(2, 2, ROWS, HD)
            rs_s[g, row, :, :, :, :HD] = key_grad.astype(BF16).reshape(2, 2, ROWS, HD)

            @pl.when(k < 3)
            def _():
                sum_y(g, k).start()

            return carry

        lax.fori_loop(0, 4, body, 0)

    def query_grads(g):
        for t in range(2):
            cols = slice(t * 768, (t + 1) * 768)
            dqh[g, cols, :] = (dot(ktr[...], dbuf[:, cols]) * SCALE).T.astype(BF16)

    def pass_far():
        pass_on(far_y(1), relays(1, zo, "f"))

    for copy in z1:
        copy.wait_recv()
    for copy in far_y(1):
        copy.start()
    heads(0)
    forward(0, pass_far)
    backward(0)
    begin_second()
    query_grads(0)
    give(0)
    heads(1)
    forward(1, lambda: None)
    reduce_y(0)
    backward(1)
    query_grads(1)
    give(1)
    reduce_y(1)
    reduce_z(0)
    for copy in second():
        copy.wait_recv()

    source = d ^ mask
    base = d - source + 2 * N_DP
    for a in range(4):
        for b in range(4):
            piece = r2[(base - (4 * a + b)) % N_DP]
            ks[b, 16 * a : 16 * a + 16, :] = piece[:, 1024:1152]
            vs[b, 16 * a : 16 * a + 16, :] = piece[:, 1152:1280]
            for j in range(GROUP):
                qs[b, j * SHORT + 16 * a : j * SHORT + 16 * a + 16, :] = piece[
                    :, j * HD : (j + 1) * HD
                ]
    width = GROUP * SHORT
    load_c.wait()
    for b in range(4):
        for j in range(GROUP):
            at = (b * GROUP + j) * HD
            cs[b, j * SHORT : (j + 1) * SHORT, :] = scb[:, at : at + HD]
    key_row = lax.broadcasted_iota(jnp.int32, (SHORT, width), 0)
    query_row = lax.broadcasted_iota(jnp.int32, (SHORT, width), 1) & (SHORT - 1)
    key_doc = jnp.zeros((SHORT, width), jnp.int32)
    query_doc = jnp.zeros((SHORT, width), jnp.int32)
    end = jnp.int32(0)
    for k in range(4):
        end = end + dl[0, k, source]
        key_doc = key_doc + jnp.where(key_row >= end, 1, 0)
        query_doc = query_doc + jnp.where(query_row >= end, 1, 0)
    allowed = (key_doc == query_doc) & (key_row <= query_row)
    for b in range(KV_HEADS):
        qt, ct, kt, vt = qs[b], cs[b], ks[b], vs[b]
        s = jnp.where(allowed, dot_nt(kt, qt) * (SCALE * LOG2E), -1e30)
        s = jnp.exp2(s - jnp.max(s, axis=0, keepdims=True))
        probs = s * (1.0 / jnp.sum(s, axis=0, keepdims=True))
        low = probs.astype(BF16)
        out = dot(vt.astype(F32).T.astype(BF16), low)
        sdvb[:, b * HD : (b + 1) * HD] = dot(low, ct).astype(BF16)
        sums = jnp.sum(out.astype(BF16).astype(F32) * ct.astype(F32).T, axis=0, keepdims=True)
        ds = (probs * (dot_nt(vt, ct) - sums)).astype(BF16)
        dq = dot(kt.astype(F32).T.astype(BF16), ds) * SCALE
        sdkb[:, b * HD : (b + 1) * HD] = (dot(ds, qt) * SCALE).astype(BF16)
        out = out.T.astype(BF16)
        dq = dq.T.astype(BF16)
        for j in range(GROUP):
            at = (b * GROUP + j) * HD
            sob[:, at : at + HD] = out[j * SHORT : (j + 1) * SHORT]
            sdqb[:, at : at + HD] = dq[j * SHORT : (j + 1) * SHORT]
    packs = [
        pltpu.make_async_copy(held, target.at[0], loc.at[10 + i])
        for i, (held, target) in enumerate(((sob, so), (sdqb, sdq), (sdkb, sdk), (sdvb, sdv)))
    ]
    for copy in packs:
        copy.start()
    reduce_z(1)
    arrived, own = [], packs
    for g in range(2):
        for copies, here in (results(g), finals(g)):
            arrived += copies
            own += here
    for copy in own:
        copy.wait()
    for copy in arrived:
        copy.wait_recv()
    for copy in waits + first() + second() + arrived:
        copy.wait_send()
    for g in range(2):
        late = relays(g, zh, "n") + relays(g, zo, "f") + far_y(g) + sums_y(g) + [sum_z(g)]
        for copy in late:
            copy.wait_send()


def write_out(*refs):
    sources, targets, held, sems = refs[:8], refs[8:16], refs[16:24], refs[24]
    first = [
        pltpu.make_async_copy(source, block, sems.at[i])
        for i, (source, block) in enumerate(zip(sources, held))
    ]
    second = [
        pltpu.make_async_copy(block, target, sems.at[8 + i])
        for i, (block, target) in enumerate(zip(held, targets))
    ]
    for copy in first:
        copy.start()
    for copy, after in zip(first, second):
        copy.wait()
        after.start()
    for copy in second:
        copy.wait()


def per_device(*args):
    any_spec = pl.BlockSpec(memory_space=pl.ANY)
    hbm = pl.BlockSpec(memory_space=pltpu.HBM)
    smem = pl.BlockSpec(memory_space=pltpu.SMEM)
    dma = pltpu.SemaphoreType.DMA
    long_query, long_key, short_query, short_key = args[0], args[1], args[5], args[6]

    args = list(args)
    args[9] = jnp.transpose(args[9], (1, 2, 0))

    def shape(like):
        return jax.ShapeDtypeStruct(like.shape, like.dtype)

    def buffer(*dims, dtype=BF16):
        return pltpu.VMEM(dims, dtype)

    results = pl.pallas_call(
        kernel,
        out_shape=(
            shape(long_query), shape(long_query), shape(long_key), shape(long_key),
            shape(short_query), shape(short_query), shape(short_key), shape(short_key),
        ),
        in_specs=[hbm] * 4 + [smem] + [hbm] * 4 + [smem] * 2,
        out_specs=(any_spec,) * 8,
        scratch_shapes=[
            buffer(ROWS, 512),
            buffer(ROWS, 512),
            buffer(SHORT, 4096),
            buffer(SHORT, 512),
            buffer(SHORT, 512),
            buffer(SHORT, 4096),
            buffer(2, 2, 4, 2, 2, ROWS, HD),
            buffer(2, 2, ROWS, HD),
            buffer(2, 2, ROWS, 1024),
            buffer(2, 2, ROWS, 1024),
            buffer(2, KEYS, HD),
            buffer(2, KEYS, HD),
            buffer(2, KEYS, HD),
            buffer(2, KEYS, HD),
            buffer(2, 2, ROWS, 1024),
            buffer(2, 2, ROWS, 1024),
            buffer(KEYS, HD),
            buffer(KEYS, HD),
            buffer(HD, KEYS),
            buffer(HD, KEYS),
            buffer(3, 1, TILE, dtype=jnp.int32),
            buffer(KEYS, PIPE * TILE, dtype=F32),
            buffer(KEYS, KEYS),
            buffer(KEYS, KEYS),
            buffer(TILES, 1, TILE, dtype=F32),
            buffer(2, 4, 2, 2, ROWS, 256),
            buffer(2, 3, 2, 2, ROWS, 256),
            buffer(2, 2, ROWS, 256, dtype=F32),
            buffer(2, 2, ROWS, 256),
            buffer(2, 2, ROWS, 256),
            buffer(2, 2, ROWS, 256),
            buffer(N_DP, 16, 1280),
            buffer(N_DP, 16, 1280),
            buffer(N_DP, 16, 1280),
            buffer(N_DP, 16, 1280),
            buffer(4, GROUP * SHORT, HD),
            buffer(4, GROUP * SHORT, HD),
            buffer(4, SHORT, HD),
            buffer(4, SHORT, HD),
            buffer(SHORT, 4096),
            buffer(SHORT, 4096),
            buffer(SHORT, 512),
            buffer(SHORT, 512),
            dma((24,)), dma((SEMS,)), dma((SEMS,)),
        ],
        compiler_params=pltpu.CompilerParams(
            collective_id=0, has_side_effects=True, vmem_limit_bytes=VMEM_LIMIT
        ),
    )(*args)
    return pl.pallas_call(
        write_out,
        out_shape=tuple(shape(result) for result in results),
        in_specs=[any_spec] * 8,
        out_specs=(hbm,) * 8,
        scratch_shapes=[buffer(*result.shape) for result in results] + [dma((16,))],
        compiler_params=pltpu.CompilerParams(vmem_limit_bytes=VMEM_LIMIT),
    )(*results)


def solution(mesh):
    wide = P("dp", "ctx", None)
    return jax.shard_map(
        per_device,
        mesh=mesh,
        in_specs=(wide,) * 4
        + (P("dp", None),)
        + (wide,) * 4
        + (P(None, "ctx", None), P("ctx", None)),
        out_specs=(wide,) * 8,
        check_vma=False,
    )
```
